32 devices in a mesh: pairs: 8 (over z, x), win: 4 (over y, core).
Axes of the slice: x: 2, y: 2, z: 4, core: 2. Of those that a mesh axis runs over, the one named last changes fastest.
Arguments:
- raw_traces: bfloat16 [4, 40, 128, 512], P('win', None, 'pairs'), may hold values from -6 to 6
- tile_pairs: int32 [8, 4, 2], replicated, may hold values from -1 to 39, as said below
- block_slot: int32 [40], replicated, may hold values from 0 to 39, as said below
- win_offset: int32 [4], P('win'), may hold values from 0 to 128
Outputs:
- stacks: float32 [128, 32, 128, 128], P('win', 'pairs')
The draws below stay inside these ranges and needn't reach their ends.
Inputs may be any that keep to these rules, and one draw needn't show every extreme that they name: `tile_pairs`: row p lists owner p's tiles: pairs of block numbers, then rows of -1. Each owner has 1 to 4 tiles and some owner exactly 4. The blocks named in one owner's row are all different. `block_slot`: each slot holds exactly one block.
All inputs are finite; a program needn't handle non-finite values.
Results may differ from the reference program's by a relative error of at most 0.0041.
Values may be sent and summed in bfloat16 or wider, within the bound.
No kernel may reach another device: no remote copies, remote signals or barrier semaphores. Data moves between devices by JAX's collectives and lax.ppermute only.
A program may use at most 192 MiB of HBM per device.

```python
import math
import jax
import jax.numpy as jnp
from jax import lax

CH = 128
NB_DEV = 5
SAMPLES = 256
LAGS = 128
TILES_DEV = 4
REC = 512
NBLK = 40
N_PAIRS = 8
N_WIN = 4


def layout_draw(key):
    block_total = NB_DEV * N_PAIRS
    block_slot = jax.random.permutation(jax.random.fold_in(key, 11), block_total).astype(jnp.int32)
    tile_tally = jax.random.randint(jax.random.fold_in(key, 12), (N_PAIRS,), 1, TILES_DEV + 1)
    fullest = jax.random.randint(jax.random.fold_in(key, 13), (), 0, N_PAIRS)
    tile_tally = jnp.where(jnp.arange(N_PAIRS) == fullest, TILES_DEV, tile_tally)
    owner_keys = jax.random.split(jax.random.fold_in(key, 14), N_PAIRS)

    def owner_blocks(owner_key):
        return jax.random.permutation(owner_key, block_total)[:2 * TILES_DEV]
    chosen = jax.vmap(owner_blocks)(owner_keys).reshape(N_PAIRS, TILES_DEV, 2)
    keep_mask = jnp.arange(TILES_DEV)[None, :] < tile_tally[:, None]
    tiles = jnp.where(keep_mask[:, :, None], chosen, -1)
    return (tiles.astype(jnp.int32), block_slot)


def draw_tile_pairs(key, part):
    return layout_draw(key)[0]


def draw_block_slot(key, part):
    return layout_draw(key)[1]


def place_ends(result, key, low, high):
    spot = [jax.random.randint(jax.random.fold_in(key, axis), (), 0, length) for axis, length in enumerate(result.shape)]
    main_axis = result.shape.index(max(result.shape))
    neighbour = spot[:main_axis] + [(spot[main_axis] + 1) % result.shape[main_axis]] + spot[main_axis + 1:]
    return result.at[tuple(spot)].set(low).at[tuple(neighbour)].set(high)


def steps_of(rng, extent, cuts, smallest, largest):
    gain, own = 1.0, jax.random.fold_in(rng, 6)
    for dim, shards_of in cuts:
        draws = jnp.exp(jax.random.uniform(jax.random.fold_in(own, dim), (shards_of,), jnp.float32, smallest / len(cuts), largest / len(cuts)))
        gain = gain * jnp.repeat(draws, extent[dim] // shards_of).reshape([-1 if axis == dim else 1 for axis in range(len(extent))])
    return gain


def noise(own_key, extent, scale, limit, cuts=(), kind=jnp.bfloat16):
    array = scale * jax.random.normal(own_key, extent, jnp.float32)
    if cuts:
        array = array * steps_of(own_key, extent, cuts, -0.22, 0.18)
    return jnp.clip(array, -limit, limit).astype(kind)


def setup_inputs(seed: int = 0) -> dict:
    key_of = jax.random.split(jax.random.key(seed), 5)
    return {
        "raw_traces": noise(key_of[0], (N_WIN, NBLK, CH, REC), 1.0, 6.0, ((0, 4), (2, 8))),
        "tile_pairs": draw_tile_pairs(jax.random.fold_in(key_of[4], 71), 0),
        "block_slot": draw_block_slot(jax.random.fold_in(key_of[4], 71), 0),
        "win_offset": place_ends(jax.random.randint(key_of[3], (N_WIN,), 0, LAGS + 1), jax.random.fold_in(key_of[3], 1), 0, LAGS).astype(jnp.int32),
    }


eps = 1e-06

def whiten(signal):
    length = signal.shape[-1]
    width = LAGS
    radius = LAGS // 2
    seg_count = length // width
    magnitude = jnp.abs(signal).reshape(signal.shape[:-1] + (seg_count, width))
    padded = jnp.pad(magnitude, [(0, 0)] * (magnitude.ndim - 2) + [(1, 1), (0, 0)])
    windows = jnp.concatenate([padded[..., :-2, :], padded[..., 1:-1, :], padded[..., 2:, :]], -1)
    rowpos = jnp.arange(3 * width)[:, None]
    colpos = jnp.arange(width)[None, :]
    band_matrix = (jnp.abs(rowpos - width - colpos) <= radius).astype(jnp.float32)
    totals = jnp.einsum('...ni,ij->...nj', windows, band_matrix, precision=lax.Precision.HIGHEST).reshape(signal.shape)
    position = jnp.arange(length)
    tally = (jnp.minimum(position, radius) + jnp.minimum(length - 1 - position, radius) + 1).astype(jnp.float32)
    return (signal / (totals / tally + eps)).astype(jnp.bfloat16)

def correlate(leading_blocks, trailing_blocks):
    seg_len = leading_blocks.shape[-1]
    samples = seg_len - LAGS
    half = LAGS // 2
    kernel = leading_blocks[..., half:half + samples].astype(jnp.float32)
    source = trailing_blocks[..., :seg_len - 1].astype(jnp.float32)
    source = jnp.transpose(source, (1, 0, 2))
    kernel = jnp.transpose(kernel, (1, 0, 2))
    return lax.conv_general_dilated(source, kernel, (1,), 'VALID', dimension_numbers=('NCH', 'OIH', 'CNH'), precision=lax.Precision.HIGHEST)

def reference(raw_traces, tile_pairs, block_slot, win_offset):
    seg_len = SAMPLES + LAGS

    def cut_window(record, offset):
        return lax.dynamic_slice_in_dim(record, offset, seg_len, 2)
    segments = jax.vmap(cut_window)(raw_traces.astype(jnp.float32), win_offset.astype(jnp.int32))
    whitened = whiten(segments)
    scale = 1.0 / math.sqrt(N_WIN * SAMPLES)
    flat_pairs = tile_pairs.reshape(-1, 2)

    def one_tile(pair):
        is_valid = pair[0] >= 0
        slot_first = block_slot[jnp.maximum(pair[0], 0)].astype(jnp.int32)
        slot_second = block_slot[jnp.maximum(pair[1], 0)].astype(jnp.int32)
        first_block = lax.dynamic_index_in_dim(whitened, slot_first, 1, keepdims=False)
        second_block = lax.dynamic_index_in_dim(whitened, slot_second, 1, keepdims=False)
        stack = correlate(first_block, second_block) * scale
        return jnp.where(is_valid, stack, jnp.zeros_like(stack))
    stacked = lax.map(one_tile, flat_pairs)
    return jnp.transpose(stacked, (1, 0, 2, 3))
```

```python
import functools
import math

import jax
import jax.numpy as jnp
from jax import lax
from jax.experimental import pallas as pl
from jax.experimental.pallas import tpu as pltpu
from jax.sharding import PartitionSpec as P

LAGS = 128
HALF = LAGS // 2
EPS = 1e-06
STEP = 16
GROUPS = ((0, 1, 2, 3), (4, 5, 6, 7))


def whiten_kernel(pairs_ref, slot_ref, offset_ref, raw_ref, *refs):
    outs, (full, lead) = refs[:-2], refs[-2:]
    _, slots, rows, rec = raw_ref.shape
    seg = rec - LAGS
    samples = seg - LAGS
    tiles = pairs_ref.shape[1]
    owner = lax.axis_index("pairs")
    band = (
        jnp.abs(
            lax.broadcasted_iota(jnp.int32, (seg, seg), 0)
            - lax.broadcasted_iota(jnp.int32, (seg, seg), 1)
        )
        <= HALF
    ).astype(jnp.bfloat16)
    position = lax.broadcasted_iota(jnp.int32, (1, seg), 1)
    tally = jnp.minimum(position, HALF) + jnp.minimum(seg - 1 - position, HALF) + 1
    inverse = 1.0 / tally.astype(jnp.float32)
    turn = lax.rem(rec - offset_ref[0], rec)
    chunk = 8

    def step(i, _):
        start = pl.multiple_of(i * chunk, chunk)
        raw = raw_ref[0, pl.ds(start, chunk)].reshape(chunk * rows, rec)
        signal = pltpu.roll(raw.astype(jnp.float32), turn, 1)[:, :seg]
        running = jnp.dot(
            jnp.abs(signal).astype(jnp.bfloat16), band, preferred_element_type=jnp.float32
        )
        whitened = signal / (running * inverse + EPS)
        full[pl.ds(start, chunk)] = whitened.astype(jnp.bfloat16).reshape(chunk, rows, seg)
        lead[pl.ds(start, chunk)] = (
            whitened[:, HALF : HALF + samples].astype(jnp.bfloat16).reshape(chunk, rows, samples)
        )
        return 0

    lax.fori_loop(0, slots // chunk, step, 0)
    for k, out in enumerate(outs):
        for t in range(tiles):
            first = slot_ref[jnp.maximum(pairs_ref[owner ^ k, t, 0], 0)]
            second = slot_ref[jnp.maximum(pairs_ref[owner ^ k, t, 1], 0)]
            out[t, :, :seg] = full[second]
            out[t, :, seg:] = lead[first]


def whiten_and_pack(raw_traces, tile_pairs, block_slot, win_offset):
    _, slots, rows, rec = raw_traces.shape
    owners, tiles, _ = tile_pairs.shape
    seg = rec - LAGS
    samples = seg - LAGS
    smem = pl.BlockSpec(memory_space=pltpu.SMEM)
    vmem = pl.BlockSpec(memory_space=pltpu.VMEM)
    return pl.pallas_call(
        whiten_kernel,
        in_specs=[smem, smem, smem, vmem],
        out_specs=[vmem] * owners,
        out_shape=[jax.ShapeDtypeStruct((tiles, rows, seg + samples), jnp.bfloat16)] * owners,
        scratch_shapes=[
            pltpu.VMEM((slots, rows, seg), jnp.bfloat16),
            pltpu.VMEM((slots, rows, samples), jnp.bfloat16),
        ],
        compiler_params=pltpu.CompilerParams(vmem_limit_bytes=24 << 20),
        name="whiten",
    )(tile_pairs, block_slot, win_offset, raw_traces)


def stack_kernel(place_ref, pairs_ref, *refs, windows, scale):
    n_in = windows * len(GROUPS)
    ins, o_ref, (block, lead, toeplitz, lagged, product) = refs[:n_in], refs[n_in], refs[n_in + 1 :]
    rows, _, chans, _ = o_ref.shape
    seg = lagged.shape[1]
    samples = seg - LAGS
    blocks = LAGS // STEP
    owner, share = place_ref[0], place_ref[1]
    tile = pl.program_id(0)
    wide = windows * samples
    n = block.shape[2]

    for w in range(windows):
        for g, group in enumerate(GROUPS):
            part = ins[g * windows + w]
            for i, k in enumerate(group):
                block[w, owner ^ k] = part[i, 0]
    for w in range(windows):
        lagged[w] = block[w, :, :, :seg].reshape(chans, seg).T
        for j in range(rows // n):
            lead[w, j * n : (j + 1) * n, :] = block[w, share * (rows // n) + j, :, seg:].astype(jnp.float32)

    def spread(c, _):
        tails = None
        at = pl.ds(pl.multiple_of(c * STEP, STEP), STEP)
        for w in range(windows):
            row = jnp.broadcast_to(lead[w, pl.ds(c, 1), :], (STEP, samples))
            row = jnp.concatenate([row, jnp.zeros((STEP, LAGS), jnp.float32)], 1)
            row = pltpu.roll(row, 0, 1, stride=1, stride_axis=0)
            toeplitz[at, w * samples : (w + 1) * samples] = row[:, :samples].astype(jnp.bfloat16)
            tail = row[:, samples:]
            if w:
                tail = pltpu.roll(tail, STEP * w, 1)
            tails = tail if tails is None else tails + tail
        toeplitz[at, wide:] = tails.astype(jnp.bfloat16)
        return 0

    lax.fori_loop(0, rows, spread, 0, unroll=4)

    for q in range(0, blocks, 2):
        halves = []
        for b in (q, q + 1):
            lo = STEP * b
            parts = [lagged[w, lo : lo + samples, :] for w in range(windows)]
            parts += [lagged[w, lo + samples : lo + samples + STEP, :] for w in range(windows)]
            parts.append(jnp.zeros((LAGS - windows * STEP, chans), jnp.bfloat16))
            halves.append(jnp.concatenate(parts, 0))
        r = jnp.dot(
            toeplitz[...], jnp.concatenate(halves, 1), preferred_element_type=jnp.float32
        )
        product[q] = r[:, :chans]
        product[q + 1] = r[:, chans:]

    factor = jnp.where(pairs_ref[owner, tile, 0] >= 0, scale, 0.0)

    def finish(c, _):
        at = pl.ds(pl.multiple_of(c * STEP, STEP), STEP)
        o_ref[c, 0] = product[:, at, :].reshape(LAGS, chans).T * factor
        return 0

    lax.fori_loop(0, rows, finish, 0, unroll=2)


def stack(place, tile_pairs, parts, windows, rows, chans, scale):
    _, tiles, n, width = parts[0].shape
    samples = (width - LAGS) // 2
    seg = samples + LAGS
    return pl.pallas_call(
        functools.partial(stack_kernel, windows=windows, scale=scale),
        grid=(tiles,),
        in_specs=[pl.BlockSpec(memory_space=pltpu.SMEM)] * 2
        + [pl.BlockSpec((p.shape[0], 1, n, width), lambda t: (0, t, 0, 0)) for p in parts],
        out_specs=pl.BlockSpec((rows, 1, chans, LAGS), lambda t: (0, t, 0, 0)),
        out_shape=jax.ShapeDtypeStruct((rows, tiles, chans, LAGS), jnp.float32),
        scratch_shapes=[
            pltpu.VMEM((windows, chans // n, n, width), jnp.bfloat16),
            pltpu.VMEM((windows, rows, samples), jnp.float32),
            pltpu.VMEM((rows * STEP, windows * samples + LAGS), jnp.bfloat16),
            pltpu.VMEM((windows, seg, chans), jnp.bfloat16),
            pltpu.VMEM((LAGS // STEP, rows * STEP, chans), jnp.float32),
        ],
        compiler_params=pltpu.CompilerParams(vmem_limit_bytes=40 << 20),
        name="stack",
    )(place, tile_pairs, *parts)


def body(raw_traces, tile_pairs, block_slot, win_offset):
    owners = lax.axis_size("pairs")
    windows = lax.axis_size("win")
    rows, rec = raw_traces.shape[2:]
    chans = rows * owners
    samples = rec - 2 * LAGS
    units = whiten_and_pack(raw_traces, tile_pairs, block_slot, win_offset)

    def swap(x, axis, size, k):
        return lax.ppermute(x, axis, [(i, i ^ k) for i in range(size)])

    units = [u if k == 0 else swap(u, "pairs", owners, k) for k, u in enumerate(units)]
    parts = []
    for group in GROUPS:
        held = jnp.stack([units[k] for k in group])
        other = swap(held, "win", windows, 2)
        parts += [held, other, swap(held, "win", windows, 1), swap(other, "win", windows, 1)]
    scale = 1.0 / math.sqrt(windows * samples)
    place = jnp.stack([lax.axis_index("pairs"), lax.axis_index("win")]).astype(jnp.int32)
    return stack(place, tile_pairs, parts, windows, chans // windows, chans, scale)


def plain_whiten(signal):
    length = signal.shape[-1]
    seg_count = length // LAGS
    magnitude = jnp.abs(signal).reshape(signal.shape[:-1] + (seg_count, LAGS))
    padded = jnp.pad(magnitude, [(0, 0)] * (magnitude.ndim - 2) + [(1, 1), (0, 0)])
    windows = jnp.concatenate([padded[..., :-2, :], padded[..., 1:-1, :], padded[..., 2:, :]], -1)
    rowpos = jnp.arange(3 * LAGS)[:, None]
    colpos = jnp.arange(LAGS)[None, :]
    band_matrix = (jnp.abs(rowpos - LAGS - colpos) <= HALF).astype(jnp.float32)
    totals = jnp.einsum(
        "...ni,ij->...nj", windows, band_matrix, precision=lax.Precision.HIGHEST
    ).reshape(signal.shape)
    position = jnp.arange(length)
    tally = (jnp.minimum(position, HALF) + jnp.minimum(length - 1 - position, HALF) + 1).astype(
        jnp.float32
    )
    return (signal / (totals / tally + EPS)).astype(jnp.bfloat16)


def plain_correlate(leading_blocks, trailing_blocks):
    seg_len = leading_blocks.shape[-1]
    samples = seg_len - LAGS
    kernel = jnp.transpose(leading_blocks[..., HALF : HALF + samples], (1, 0, 2))
    source = jnp.transpose(trailing_blocks[..., : seg_len - 1], (1, 0, 2))
    return lax.conv_general_dilated(
        source,
        kernel,
        (1,),
        "VALID",
        dimension_numbers=("NCH", "OIH", "CNH"),
        preferred_element_type=jnp.float32,
    )


def plain_body(raw_traces, tile_pairs, block_slot, win_offset):
    owner_index = lax.axis_index("pairs")
    pair_count = lax.axis_size("pairs")
    win_count = lax.axis_size("win")
    local_channels = raw_traces.shape[2]
    channels = local_channels * pair_count
    seg_len = raw_traces.shape[3] - LAGS
    samples = seg_len - LAGS
    tile_count = tile_pairs.shape[1]
    segment = lax.dynamic_slice_in_dim(raw_traces[0], win_offset[0], seg_len, 2).astype(jnp.float32)
    whitened = plain_whiten(segment)
    wanted = tile_pairs.reshape(pair_count, 2 * tile_count)
    slot_index = block_slot[jnp.maximum(wanted, 0)]
    outgoing = jnp.take(whitened, slot_index.reshape(-1), axis=0).reshape(
        pair_count, 2 * tile_count, local_channels, seg_len
    )
    incoming = lax.all_to_all(outgoing, "pairs", split_axis=0, concat_axis=2, tiled=True)
    blocks = incoming[0].reshape(tile_count, 2, channels, seg_len)
    own_tiles = lax.dynamic_index_in_dim(tile_pairs, owner_index, 0, keepdims=False)
    tile_valid = (own_tiles[:, 0] >= 0).astype(jnp.float32)
    firsts = blocks[:, 0]
    seconds = blocks[:, 1]
    spread_rows = lax.all_to_all(firsts[:, None], "win", split_axis=2, concat_axis=1, tiled=True)
    piece = lax.all_gather(seconds[:, None], "win", axis=1, tiled=True)
    summed = jnp.stack(
        [plain_correlate(spread_rows[tile], piece[tile]) for tile in range(tile_count)], 1
    )
    scale = 1.0 / math.sqrt(win_count * samples)
    return summed * scale * tile_valid[None, :, None, None]


def solution(mesh):
    regular = mesh.shape["pairs"] == 8 and mesh.shape["win"] == 4
    return jax.shard_map(
        body if regular else plain_body,
        mesh=mesh,
        in_specs=(P("win", None, "pairs", None), P(), P(), P("win")),
        out_specs=P("win", "pairs", None, None),
        check_vma=False,
    )
```

```python
import functools
import math

import jax
import jax.numpy as jnp
from jax import lax
from jax.experimental import pallas as pl
from jax.experimental.pallas import tpu as pltpu
from jax.sharding import PartitionSpec as P

LAGS = 128
HALF = LAGS // 2
EPS = 1e-06
STEP = 16


def whiten_kernel(pairs_ref, slot_ref, offset_ref, raw_ref, *refs):
    outs, (full, lead) = refs[:-2], refs[-2:]
    _, slots, rows, rec = raw_ref.shape
    seg = rec - LAGS
    samples = seg - LAGS
    tiles = pairs_ref.shape[1]
    owner = lax.axis_index("pairs")
    band = (
        jnp.abs(
            lax.broadcasted_iota(jnp.int32, (seg, seg), 0)
            - lax.broadcasted_iota(jnp.int32, (seg, seg), 1)
        )
        <= HALF
    ).astype(jnp.bfloat16)
    position = lax.broadcasted_iota(jnp.int32, (1, seg), 1)
    tally = jnp.minimum(position, HALF) + jnp.minimum(seg - 1 - position, HALF) + 1
    inverse = 1.0 / tally.astype(jnp.float32)
    turn = lax.rem(rec - offset_ref[0], rec)
    chunk = 8

    def step(i, _):
        start = pl.multiple_of(i * chunk, chunk)
        raw = raw_ref[0, pl.ds(start, chunk)].reshape(chunk * rows, rec)
        signal = pltpu.roll(raw.astype(jnp.float32), turn, 1)[:, :seg]
        running = jnp.dot(
            jnp.abs(signal).astype(jnp.bfloat16), band, preferred_element_type=jnp.float32
        )
        whitened = signal / (running * inverse + EPS)
        full[pl.ds(start, chunk)] = whitened.astype(jnp.bfloat16).reshape(chunk, rows, seg)
        lead[pl.ds(start, chunk)] = (
            whitened[:, HALF : HALF + samples].astype(jnp.bfloat16).reshape(chunk, rows, samples)
        )
        return 0

    lax.fori_loop(0, slots // chunk, step, 0)
    for k, out in enumerate(outs):
        for t in range(tiles):
            first = slot_ref[jnp.maximum(pairs_ref[owner ^ k, t, 0], 0)]
            second = slot_ref[jnp.maximum(pairs_ref[owner ^ k, t, 1], 0)]
            out[t, :, :seg] = full[second]
            out[t, :, seg:] = lead[first]


def whiten_and_pack(raw_traces, tile_pairs, block_slot, win_offset):
    _, slots, rows, rec = raw_traces.shape
    owners, tiles, _ = tile_pairs.shape
    seg = rec - LAGS
    samples = seg - LAGS
    smem = pl.BlockSpec(memory_space=pltpu.SMEM)
    vmem = pl.BlockSpec(memory_space=pltpu.VMEM)
    return pl.pallas_call(
        whiten_kernel,
        in_specs=[smem, smem, smem, vmem],
        out_specs=[vmem] * owners,
        out_shape=[jax.ShapeDtypeStruct((tiles, rows, seg + samples), jnp.bfloat16)] * owners,
        scratch_shapes=[
            pltpu.VMEM((slots, rows, seg), jnp.bfloat16),
            pltpu.VMEM((slots, rows, samples), jnp.bfloat16),
        ],
        compiler_params=pltpu.CompilerParams(vmem_limit_bytes=24 << 20),
        name="whiten",
    )(tile_pairs, block_slot, win_offset, raw_traces)


def stack_kernel(place_ref, pairs_ref, *refs, windows, scale):
    n_in = 2 * windows
    ins, out_ref = refs[:n_in], refs[n_in]
    far, near = ins[:windows], ins[windows:]
    lead, ends, *pairs_of, done = refs[n_in + 1 :]
    toeplitz, lagged, product, staged = (pairs_of[i : i + 2] for i in range(0, 8, 2))
    rows, tiles, chans, _ = out_ref.shape
    half, _, n, _ = near[0].shape
    seg = lagged[0].shape[1]
    samples = seg - LAGS
    wide = windows * samples
    blocks = LAGS // STEP
    rounds = blocks // 2
    per = rows // rounds
    owner, share = place_ref[0], place_ref[1]
    lane = lax.broadcasted_iota(jnp.int32, (STEP, LAGS), 1)
    shift = lax.broadcasted_iota(jnp.int32, (STEP, LAGS), 0)
    early = lane < shift
    tail = (lax.rem(lane, STEP) < shift) & (lane < windows * STEP)

    def unit(w, t, j, lanes):
        k = owner ^ j
        here = (k < half).astype(jnp.int32) * jnp.ones((n, 1), jnp.int32) > 0
        at = k & (half - 1)
        return jnp.where(here, near[w][at, t, :, lanes], far[w][at, t, :, lanes])

    def prepare(t, s):
        lanes = lax.broadcasted_iota(jnp.int32, (rows, LAGS), 1)
        last = jnp.zeros((rows, LAGS), jnp.float32)
        for w in range(windows):
            second = [unit(w, t, j, slice(0, seg)) for j in range(2 * half)]
            lagged[s][w] = jnp.concatenate(second, 0).T
            first = [
                unit(w, t, share * (rows // n) + j, slice(seg, seg + samples))
                for j in range(rows // n)
            ]
            mine = jnp.concatenate(first, 0).astype(jnp.float32)
            lead[w] = mine
            at = (w - 1) * STEP % LAGS
            last += jnp.where(
                (lanes >= at) & (lanes < at + STEP),
                pltpu.roll(mine[:, samples - LAGS :], w * STEP, 1) if w else mine[:, samples - LAGS :],
                0.0,
            )
        ends[...] = last

    def turned(row):
        return pltpu.roll(jnp.broadcast_to(row, (STEP, LAGS)), 0, 1, stride=1, stride_axis=0)

    def spread(c, s):
        at = pl.ds(pl.multiple_of(c * STEP, STEP), STEP)
        for w in range(windows):
            before = None
            row = lead[w, pl.ds(c, 1), :]
            for lo in range(0, samples, LAGS):
                now = turned(row[:, lo : lo + LAGS])
                fill = 0.0 if before is None else before
                toeplitz[s][at, w * samples + lo : w * samples + lo + LAGS] = jnp.where(
                    early, fill, now
                ).astype(jnp.bfloat16)
                before = now
        toeplitz[s][at, wide:] = jnp.where(tail, turned(ends[pl.ds(c, 1), :]), 0.0).astype(jnp.bfloat16)

    def multiply(q, s):
        halves = []
        for b in range(2):
            lo = (2 * q + b) * STEP
            lo = lo if isinstance(lo, int) else pl.multiple_of(lo, STEP)
            parts = [lagged[s][w, pl.ds(lo, samples), :] for w in range(windows)]
            parts += [lagged[s][w, pl.ds(lo + samples, STEP), :] for w in range(windows)]
            parts.append(jnp.zeros((LAGS - windows * STEP, chans), jnp.bfloat16))
            halves.append(jnp.concatenate(parts, 0))
        r = jnp.dot(
            toeplitz[s][...], jnp.concatenate(halves, 1), preferred_element_type=jnp.float32
        )
        product[s][2 * q] = r[:, :chans]
        product[s][2 * q + 1] = r[:, chans:]

    def finish(c, s, factor):
        at = pl.ds(pl.multiple_of(c * STEP, STEP), STEP)
        staged[s][c] = product[s][:, at, :].reshape(LAGS, chans).T * factor

    def copy(t):
        return pltpu.make_async_copy(staged[t % 2], out_ref.at[:, t], done.at[t % 2])

    for t in range(-1, tiles + 1):
        if t + 1 < tiles:
            prepare(t + 1, (t + 1) % 2)
        if t >= 1:
            factor = jnp.where(pairs_ref[owner, t - 1, 0] >= 0, scale, 0.0)
            if t >= 3:
                copy(t - 3).wait()

        def step(q, _):
            if 0 <= t < tiles:
                multiply(q, t % 2)
            for i in range(per):
                if t + 1 < tiles:
                    spread(q * per + i, (t + 1) % 2)
                if t >= 1:
                    finish(q * per + i, (t - 1) % 2, factor)
            return 0

        lax.fori_loop(0, rounds, step, 0, unroll=True)
        if t >= 1:
            copy(t - 1).start()
    for t in range(max(tiles - 2, 0), tiles):
        copy(t).wait()


def stack(place, tile_pairs, parts, windows, rows, chans, scale):
    _, tiles, n, width = parts[0].shape
    samples = (width - LAGS) // 2
    seg = samples + LAGS
    smem = pl.BlockSpec(memory_space=pltpu.SMEM)
    vmem = pl.BlockSpec(memory_space=pltpu.VMEM)
    return pl.pallas_call(
        functools.partial(stack_kernel, windows=windows, scale=scale),
        in_specs=[smem] * 2 + [vmem] * len(parts),
        out_specs=pl.BlockSpec(memory_space=pl.ANY),
        out_shape=jax.ShapeDtypeStruct((rows, tiles, chans, LAGS), jnp.float32),
        scratch_shapes=[
            pltpu.VMEM((windows, rows, samples), jnp.float32),
            pltpu.VMEM((rows, LAGS), jnp.float32),
        ]
        + [pltpu.VMEM((rows * STEP, windows * samples + LAGS), jnp.bfloat16)] * 2
        + [pltpu.VMEM((windows, seg, chans), jnp.bfloat16)] * 2
        + [pltpu.VMEM((LAGS // STEP, rows * STEP, chans), jnp.float32)] * 2
        + [pltpu.VMEM((rows, chans, LAGS), jnp.float32)] * 2
        + [pltpu.SemaphoreType.DMA((2,))],
        compiler_params=pltpu.CompilerParams(vmem_limit_bytes=40 << 20),
        name="stack",
    )(place, tile_pairs, *parts)


def body(raw_traces, tile_pairs, block_slot, win_offset):
    owners = lax.axis_size("pairs")
    windows = lax.axis_size("win")
    rows, rec = raw_traces.shape[2:]
    chans = rows * owners
    samples = rec - 2 * LAGS
    units = whiten_and_pack(raw_traces, tile_pairs, block_slot, win_offset)

    def swap(x, axis, size, k):
        return lax.ppermute(x, axis, [(i, i ^ k) for i in range(size)])

    units = [u if k == 0 else swap(u, "pairs", owners, k) for k, u in enumerate(units)]
    parts = []
    for low in (owners // 2, 0):
        held = jnp.stack(units[low : low + owners // 2])
        other = swap(held, "win", windows, 2)
        parts += [held, other, swap(held, "win", windows, 1), swap(other, "win", windows, 1)]
    scale = 1.0 / math.sqrt(windows * samples)
    place = jnp.stack([lax.axis_index("pairs"), lax.axis_index("win")]).astype(jnp.int32)
    return stack(place, tile_pairs, parts, windows, chans // windows, chans, scale)


def plain_whiten(signal):
    length = signal.shape[-1]
    seg_count = length // LAGS
    magnitude = jnp.abs(signal).reshape(signal.shape[:-1] + (seg_count, LAGS))
    padded = jnp.pad(magnitude, [(0, 0)] * (magnitude.ndim - 2) + [(1, 1), (0, 0)])
    windows = jnp.concatenate([padded[..., :-2, :], padded[..., 1:-1, :], padded[..., 2:, :]], -1)
    rowpos = jnp.arange(3 * LAGS)[:, None]
    colpos = jnp.arange(LAGS)[None, :]
    band_matrix = (jnp.abs(rowpos - LAGS - colpos) <= HALF).astype(jnp.float32)
    totals = jnp.einsum(
        "...ni,ij->...nj", windows, band_matrix, precision=lax.Precision.HIGHEST
    ).reshape(signal.shape)
    position = jnp.arange(length)
    tally = (jnp.minimum(position, HALF) + jnp.minimum(length - 1 - position, HALF) + 1).astype(
        jnp.float32
    )
    return (signal / (totals / tally + EPS)).astype(jnp.bfloat16)


def plain_correlate(leading_blocks, trailing_blocks):
    seg_len = leading_blocks.shape[-1]
    samples = seg_len - LAGS
    kernel = jnp.transpose(leading_blocks[..., HALF : HALF + samples], (1, 0, 2))
    source = jnp.transpose(trailing_blocks[..., : seg_len - 1], (1, 0, 2))
    return lax.conv_general_dilated(
        source,
        kernel,
        (1,),
        "VALID",
        dimension_numbers=("NCH", "OIH", "CNH"),
        preferred_element_type=jnp.float32,
    )


def plain_body(raw_traces, tile_pairs, block_slot, win_offset):
    owner_index = lax.axis_index("pairs")
    pair_count = lax.axis_size("pairs")
    win_count = lax.axis_size("win")
    local_channels = raw_traces.shape[2]
    channels = local_channels * pair_count
    seg_len = raw_traces.shape[3] - LAGS
    samples = seg_len - LAGS
    tile_count = tile_pairs.shape[1]
    segment = lax.dynamic_slice_in_dim(raw_traces[0], win_offset[0], seg_len, 2).astype(jnp.float32)
    whitened = plain_whiten(segment)
    wanted = tile_pairs.reshape(pair_count, 2 * tile_count)
    slot_index = block_slot[jnp.maximum(wanted, 0)]
    outgoing = jnp.take(whitened, slot_index.reshape(-1), axis=0).reshape(
        pair_count, 2 * tile_count, local_channels, seg_len
    )
    incoming = lax.all_to_all(outgoing, "pairs", split_axis=0, concat_axis=2, tiled=True)
    blocks = incoming[0].reshape(tile_count, 2, channels, seg_len)
    own_tiles = lax.dynamic_index_in_dim(tile_pairs, owner_index, 0, keepdims=False)
    tile_valid = (own_tiles[:, 0] >= 0).astype(jnp.float32)
    firsts = blocks[:, 0]
    seconds = blocks[:, 1]
    spread_rows = lax.all_to_all(firsts[:, None], "win", split_axis=2, concat_axis=1, tiled=True)
    piece = lax.all_gather(seconds[:, None], "win", axis=1, tiled=True)
    summed = jnp.stack(
        [plain_correlate(spread_rows[tile], piece[tile]) for tile in range(tile_count)], 1
    )
    scale = 1.0 / math.sqrt(win_count * samples)
    return summed * scale * tile_valid[None, :, None, None]


def solution(mesh):
    regular = mesh.shape["pairs"] == 8 and mesh.shape["win"] == 4
    return jax.shard_map(
        body if regular else plain_body,
        mesh=mesh,
        in_specs=(P("win", None, "pairs", None), P(), P(), P("win")),
        out_specs=P("win", "pairs", None, None),
        check_vma=False,
    )
```

```python
import functools
import math

import jax
import jax.numpy as jnp
from jax import lax
from jax.experimental import pallas as pl
from jax.experimental.pallas import tpu as pltpu
from jax.sharding import PartitionSpec as P

LAGS = 128
HALF = LAGS // 2
EPS = 1e-06
STEP = 16
WHITEN_VMEM = 60 << 20


def whiten_kernel(pairs_hbm, slot_hbm, offset_hbm, raw_hbm, *refs, scale):
    *outs, factor_ref, raw_ref, full, lead, pairs_ref, slot_ref, offset_ref, small, large = refs
    slots, rows, rec = raw_ref.shape
    seg = rec - LAGS
    samples = seg - LAGS
    tiles = pairs_ref.shape[0]
    chunk = 8
    scalars = [
        pltpu.make_async_copy(src, dst, small.at[i])
        for i, (src, dst) in enumerate(
            ((offset_hbm, offset_ref), (pairs_hbm, pairs_ref), (slot_hbm, slot_ref))
        )
    ]
    pieces = [
        pltpu.make_async_copy(
            raw_hbm.at[0, pl.ds(lo, chunk)], raw_ref.at[pl.ds(lo, chunk)], large.at[lo // chunk]
        )
        for lo in range(0, slots, chunk)
    ]
    for one in scalars + pieces:
        one.start()
    owner = lax.axis_index("pairs")
    band = (
        jnp.abs(
            lax.broadcasted_iota(jnp.int32, (seg, seg), 0)
            - lax.broadcasted_iota(jnp.int32, (seg, seg), 1)
        )
        <= HALF
    ).astype(jnp.bfloat16)
    position = lax.broadcasted_iota(jnp.int32, (1, seg), 1)
    tally = jnp.minimum(position, HALF) + jnp.minimum(seg - 1 - position, HALF) + 1
    inverse = 1.0 / tally.astype(jnp.float32)
    scalars[0].wait()
    turn = lax.rem(rec - offset_ref[0], rec)
    for i, piece in enumerate(pieces):
        piece.wait()
        at = slice(i * chunk, (i + 1) * chunk)
        raw = raw_ref[at].reshape(chunk * rows, rec)
        signal = pltpu.roll(raw.astype(jnp.float32), turn, 1)[:, :seg]
        running = jnp.dot(
            jnp.abs(signal).astype(jnp.bfloat16), band, preferred_element_type=jnp.float32
        )
        whitened = signal / (running * inverse + EPS)
        full[at] = whitened.astype(jnp.bfloat16).reshape(chunk, rows, seg)
        lead[at] = (
            whitened[:, HALF : HALF + samples].astype(jnp.bfloat16).reshape(chunk, rows, samples)
        )
    scalars[1].wait()
    scalars[2].wait()
    for t in range(tiles):
        used = jnp.where(pairs_ref[t, 0, owner] >= 0, scale, 0.0)
        factor_ref[t] = jnp.full(factor_ref.shape[1:], used, jnp.float32)
    for k, out in enumerate(outs):
        for t in range(tiles):
            first = slot_ref[jnp.maximum(pairs_ref[t, 0, owner ^ k], 0)]
            second = slot_ref[jnp.maximum(pairs_ref[t, 1, owner ^ k], 0)]
            out[t, :, :seg] = full[second]
            out[t, :, seg:] = lead[first]


def whiten_and_pack(raw_traces, pairs_last, block_slot, win_offset, scale):
    _, slots, rows, rec = raw_traces.shape
    tiles, _, owners = pairs_last.shape
    seg = rec - LAGS
    samples = seg - LAGS
    vmem = pl.BlockSpec(memory_space=pltpu.VMEM)
    return pl.pallas_call(
        functools.partial(whiten_kernel, scale=scale),
        in_specs=[pl.BlockSpec(memory_space=pl.ANY)] * 4,
        out_specs=[vmem] * (owners + 1),
        out_shape=[jax.ShapeDtypeStruct((tiles, rows, seg + samples), jnp.bfloat16)] * owners
        + [jax.ShapeDtypeStruct((tiles, 8, LAGS), jnp.float32)],
        scratch_shapes=[
            pltpu.VMEM((slots, rows, rec), jnp.bfloat16),
            pltpu.VMEM((slots, rows, seg), jnp.bfloat16),
            pltpu.VMEM((slots, rows, samples), jnp.bfloat16),
            pltpu.SMEM(pairs_last.shape, jnp.int32),
            pltpu.SMEM(block_slot.shape, jnp.int32),
            pltpu.SMEM(win_offset.shape, jnp.int32),
            pltpu.SemaphoreType.DMA((3,)),
            pltpu.SemaphoreType.DMA((slots // 8,)),
        ],
        compiler_params=pltpu.CompilerParams(vmem_limit_bytes=WHITEN_VMEM),
        name="whiten",
    )(pairs_last, block_slot, win_offset, raw_traces)


def unit(far, near, owner, t, j, lanes):
    half, _, n, _ = near.shape
    k = owner ^ j
    here = (k < half).astype(jnp.int32) * jnp.ones((n, 1), jnp.int32) > 0
    at = k & (half - 1)
    return jnp.where(here, near[at, t, :, lanes], far[at, t, :, lanes])


def second_block(far, near, owner, t, lanes):
    return jnp.concatenate(
        [unit(far, near, owner, t, j, lanes) for j in range(2 * near.shape[0])], 0
    )


def first_rows(far, near, owner, share, t, rows, lanes):
    n = near.shape[2]
    return jnp.concatenate(
        [unit(far, near, owner, t, share * (rows // n) + j, lanes) for j in range(rows // n)], 0
    )


def turned(row):
    return pltpu.roll(jnp.broadcast_to(row, (STEP, LAGS)), 0, 1, stride=1, stride_axis=0)


def spread(c, lead, toeplitz, windows, samples):
    lane = lax.broadcasted_iota(jnp.int32, (STEP, LAGS), 1)
    early = lane < lax.broadcasted_iota(jnp.int32, (STEP, LAGS), 0)
    at = pl.ds(pl.multiple_of(c * STEP, STEP), STEP)
    for w in range(windows):
        before = 0.0
        row = lead[w, pl.ds(c, 1), :]
        for lo in range(0, samples, LAGS):
            now = turned(row[:, lo : lo + LAGS])
            toeplitz[at, w * samples + lo : w * samples + lo + LAGS] = jnp.where(
                early, before, now
            ).astype(jnp.bfloat16)
            before = now


def held_kernel(*refs, windows):
    far, near = refs[:windows], refs[windows : 2 * windows]
    out_ref, lead, *pairs_of = refs[2 * windows :]
    toeplitz, lagged = pairs_of[:2], pairs_of[2:]
    tiles, blocks, _, chans = out_ref.shape
    _, rows, samples = lead.shape
    seg = samples + LAGS
    rounds = blocks // 2
    per = rows // rounds
    owner, share = lax.axis_index("pairs"), lax.axis_index("win")
    for t in range(-1, tiles):
        if t + 1 < tiles:
            for w in range(windows):
                block = second_block(far[w], near[w], owner, t + 1, slice(0, seg))
                lagged[(t + 1) % 2][w] = block.T
                mine = first_rows(far[w], near[w], owner, share, t + 1, rows, slice(seg, None))
                lead[w] = mine.astype(jnp.float32)

        def step(q, _):
            if t >= 0:
                halves = []
                for b in range(2):
                    lo = pl.multiple_of((2 * q + b) * STEP, STEP)
                    parts = [lagged[t % 2][w, pl.ds(lo, samples), :] for w in range(windows)]
                    halves.append(jnp.concatenate(parts, 0))
                r = jnp.dot(
                    toeplitz[t % 2][...],
                    jnp.concatenate(halves, 1),
                    preferred_element_type=jnp.float32,
                )
                out_ref[t, 2 * q] = r[:, :chans]
                out_ref[t, 2 * q + 1] = r[:, chans:]
            if t + 1 < tiles:
                for i in range(per):
                    spread(q * per + i, lead, toeplitz[(t + 1) % 2], windows, samples)
            return 0

        lax.fori_loop(0, rounds, step, 0, unroll=True)


def stack_kernel(factor_hbm, *refs, windows):
    ins, sums, out_ref = refs[: 2 * windows], refs[2 * windows], refs[2 * windows + 1]
    far, near = ins[:windows], ins[windows:]
    lead, ends, *pairs_of, factor_ref, done, ready = refs[2 * windows + 2 :]
    toeplitz, lagged, lasting, product, staged = (pairs_of[i : i + 2] for i in range(0, 10, 2))
    rows, tiles, chans, _ = out_ref.shape
    new, _, samples = lead.shape
    seg = samples + LAGS
    wide = new * samples
    blocks = LAGS // STEP
    rounds = blocks // 2
    per = rows // rounds
    owner, share = lax.axis_index("pairs"), lax.axis_index("win")
    lane = lax.broadcasted_iota(jnp.int32, (STEP, LAGS), 1)
    shift = lax.broadcasted_iota(jnp.int32, (STEP, LAGS), 0)
    tail = (lax.rem(lane, STEP) < shift) & (lane < windows * STEP)
    factors = pltpu.make_async_copy(factor_hbm, factor_ref, ready.at[0])
    factors.start()

    def prepare(t, s):
        lanes = lax.broadcasted_iota(jnp.int32, (rows, LAGS), 1)
        last = jnp.zeros((rows, LAGS), jnp.float32)
        for w in range(windows):
            fresh = w - (windows - new)
            if fresh >= 0:
                lagged[s][fresh] = second_block(far[w], near[w], owner, t, slice(0, samples)).T
                mine = first_rows(
                    far[w], near[w], owner, share, t, rows, slice(seg, seg + samples)
                ).astype(jnp.float32)
                lead[fresh] = mine
                mine = mine[:, samples - LAGS :]
            else:
                mine = first_rows(
                    far[w], near[w], owner, share, t, rows, slice(2 * samples, None)
                ).astype(jnp.float32)
            lasting[s][w] = second_block(far[w], near[w], owner, t, slice(samples, seg)).T
            at = (w - 1) * STEP % LAGS
            last += jnp.where(
                (lanes >= at) & (lanes < at + STEP),
                pltpu.roll(mine, w * STEP, 1) if w else mine,
                0.0,
            )
        ends[...] = last

    def multiply(q, t, s):
        halves = []
        for b in range(2):
            lo = (2 * q + b) * STEP
            parts = []
            for w in range(new):
                parts += [lagged[s][w, lo:, :], lasting[s][windows - new + w, :lo, :]]
            parts += [lasting[s][w, lo : lo + STEP, :] for w in range(windows)]
            parts.append(jnp.zeros((LAGS - windows * STEP, chans), jnp.bfloat16))
            halves.append(jnp.concatenate([p for p in parts if p.shape[0]], 0))
        r = jnp.dot(
            toeplitz[s][...], jnp.concatenate(halves, 1), preferred_element_type=jnp.float32
        )
        product[s][2 * q] = r[:, :chans] + sums[t, 2 * q]
        product[s][2 * q + 1] = r[:, chans:] + sums[t, 2 * q + 1]

    def finish(c, s, factor):
        at = pl.ds(c * STEP, STEP)
        staged[s][c] = product[s][:, at, :].reshape(LAGS, chans).T * factor

    def copy(t):
        return pltpu.make_async_copy(staged[t % 2], out_ref.at[:, t], done.at[t % 2])

    for t in range(-1, tiles + 1):
        if t + 1 < tiles:
            prepare(t + 1, (t + 1) % 2)
        if t == 1:
            factors.wait()
        if t >= 1:
            factor = factor_ref[t - 1, 0:1, :]
            if t >= 3:
                copy(t - 3).wait()
        for q in range(rounds):
            if 0 <= t < tiles:
                multiply(q, t, t % 2)
            for c in range(q * per, (q + 1) * per):
                if t + 1 < tiles:
                    spread(c, lead, toeplitz[(t + 1) % 2], new, samples)
                    toeplitz[(t + 1) % 2][c * STEP : (c + 1) * STEP, wide:] = jnp.where(
                        tail, turned(ends[c : c + 1, :]), 0.0
                    ).astype(jnp.bfloat16)
                if t >= 1:
                    finish(c, (t - 1) % 2, factor)
        if t >= 1:
            copy(t - 1).start()
    for t in range(max(tiles - 2, 0), tiles):
        copy(t).wait()


def stack(factor, held, brought, rows, chans):
    _, tiles, n, width = held[0][0].shape
    samples = (width - LAGS) // 2
    seg = samples + LAGS
    depth = rows * STEP
    windows, old, new = len(held) + len(brought), len(held), len(brought)
    vmem = pl.BlockSpec(memory_space=pltpu.VMEM)
    hbm = pl.BlockSpec(memory_space=pl.ANY)

    def flat(groups):
        return [g[0] for g in groups] + [g[1] for g in groups]

    flops = 2 * tiles * depth * samples * chans * (LAGS // STEP)
    sums = pl.pallas_call(
        functools.partial(held_kernel, windows=old),
        in_specs=[vmem] * (2 * old),
        out_specs=vmem,
        out_shape=jax.ShapeDtypeStruct((tiles, LAGS // STEP, depth, chans), jnp.float32),
        scratch_shapes=[pltpu.VMEM((old, rows, samples), jnp.float32)]
        + [pltpu.VMEM((depth, old * samples), jnp.bfloat16)] * 2
        + [pltpu.VMEM((old, seg, chans), jnp.bfloat16)] * 2,
        compiler_params=pltpu.CompilerParams(vmem_limit_bytes=24 << 20),
        cost_estimate=pl.CostEstimate(
            flops=old * flops, bytes_accessed=8 << 20, transcendentals=0
        ),
        name="held",
    )(*flat(held))
    return pl.pallas_call(
        functools.partial(stack_kernel, windows=windows),
        in_specs=[hbm] + [vmem] * (2 * windows + 1),
        out_specs=hbm,
        out_shape=jax.ShapeDtypeStruct((rows, tiles, chans, LAGS), jnp.float32),
        scratch_shapes=[
            pltpu.VMEM((new, rows, samples), jnp.float32),
            pltpu.VMEM((rows, LAGS), jnp.float32),
        ]
        + [pltpu.VMEM((depth, new * samples + LAGS), jnp.bfloat16)] * 2
        + [pltpu.VMEM((new, samples, chans), jnp.bfloat16)] * 2
        + [pltpu.VMEM((windows, LAGS, chans), jnp.bfloat16)] * 2
        + [pltpu.VMEM((LAGS // STEP, depth, chans), jnp.float32)] * 2
        + [pltpu.VMEM((rows, chans, LAGS), jnp.float32)] * 2
        + [
            pltpu.VMEM(factor.shape, jnp.float32),
            pltpu.SemaphoreType.DMA((2,)),
            pltpu.SemaphoreType.DMA((1,)),
        ],
        compiler_params=pltpu.CompilerParams(vmem_limit_bytes=24 << 20),
        name="stack",
    )(factor, *flat(held + brought), sums)


def body(raw_traces, tile_pairs, block_slot, win_offset):
    owners = lax.axis_size("pairs")
    windows = lax.axis_size("win")
    rows, rec = raw_traces.shape[2:]
    chans = rows * owners
    samples = rec - 2 * LAGS
    pairs_last = jnp.transpose(tile_pairs, (1, 2, 0))
    scale = 1.0 / math.sqrt(windows * samples)
    *units, factor = whiten_and_pack(raw_traces, pairs_last, block_slot, win_offset, scale)

    def swap(x, axis, size, k):
        return lax.ppermute(x, axis, [(i, i ^ k) for i in range(size)])

    units = [u if k == 0 else swap(u, "pairs", owners, k) for k, u in enumerate(units)]
    held, brought = [], []
    for low in (owners // 2, 0):
        own = jnp.stack(units[low : low + owners // 2])
        other = swap(own, "win", windows, 2)
        held.append((own, swap(own, "win", windows, 1)))
        brought.append((other, swap(other, "win", windows, 1)))
    return stack(factor, list(zip(*held)), list(zip(*brought)), chans // windows, chans)


def plain_whiten(signal):
    length = signal.shape[-1]
    seg_count = length // LAGS
    magnitude = jnp.abs(signal).reshape(signal.shape[:-1] + (seg_count, LAGS))
    padded = jnp.pad(magnitude, [(0, 0)] * (magnitude.ndim - 2) + [(1, 1), (0, 0)])
    windows = jnp.concatenate([padded[..., :-2, :], padded[..., 1:-1, :], padded[..., 2:, :]], -1)
    rowpos = jnp.arange(3 * LAGS)[:, None]
    colpos = jnp.arange(LAGS)[None, :]
    band_matrix = (jnp.abs(rowpos - LAGS - colpos) <= HALF).astype(jnp.float32)
    totals = jnp.einsum(
        "...ni,ij->...nj", windows, band_matrix, precision=lax.Precision.HIGHEST
    ).reshape(signal.shape)
    position = jnp.arange(length)
    tally = (jnp.minimum(position, HALF) + jnp.minimum(length - 1 - position, HALF) + 1).astype(
        jnp.float32
    )
    return (signal / (totals / tally + EPS)).astype(jnp.bfloat16)


def plain_correlate(leading_blocks, trailing_blocks):
    seg_len = leading_blocks.shape[-1]
    samples = seg_len - LAGS
    kernel = jnp.transpose(leading_blocks[..., HALF : HALF + samples], (1, 0, 2))
    source = jnp.transpose(trailing_blocks[..., : seg_len - 1], (1, 0, 2))
    return lax.conv_general_dilated(
        source,
        kernel,
        (1,),
        "VALID",
        dimension_numbers=("NCH", "OIH", "CNH"),
        preferred_element_type=jnp.float32,
    )


def plain_body(raw_traces, tile_pairs, block_slot, win_offset):
    owner_index = lax.axis_index("pairs")
    pair_count = lax.axis_size("pairs")
    win_count = lax.axis_size("win")
    local_channels = raw_traces.shape[2]
    channels = local_channels * pair_count
    seg_len = raw_traces.shape[3] - LAGS
    samples = seg_len - LAGS
    tile_count = tile_pairs.shape[1]
    segment = lax.dynamic_slice_in_dim(raw_traces[0], win_offset[0], seg_len, 2).astype(jnp.float32)
    whitened = plain_whiten(segment)
    wanted = tile_pairs.reshape(pair_count, 2 * tile_count)
    slot_index = block_slot[jnp.maximum(wanted, 0)]
    outgoing = jnp.take(whitened, slot_index.reshape(-1), axis=0).reshape(
        pair_count, 2 * tile_count, local_channels, seg_len
    )
    incoming = lax.all_to_all(outgoing, "pairs", split_axis=0, concat_axis=2, tiled=True)
    blocks = incoming[0].reshape(tile_count, 2, channels, seg_len)
    own_tiles = lax.dynamic_index_in_dim(tile_pairs, owner_index, 0, keepdims=False)
    tile_valid = (own_tiles[:, 0] >= 0).astype(jnp.float32)
    firsts = blocks[:, 0]
    seconds = blocks[:, 1]
    spread_rows = lax.all_to_all(firsts[:, None], "win", split_axis=2, concat_axis=1, tiled=True)
    piece = lax.all_gather(seconds[:, None], "win", axis=1, tiled=True)
    summed = jnp.stack(
        [plain_correlate(spread_rows[tile], piece[tile]) for tile in range(tile_count)], 1
    )
    scale = 1.0 / math.sqrt(win_count * samples)
    return summed * scale * tile_valid[None, :, None, None]


def solution(mesh):
    regular = mesh.shape["pairs"] == 8 and mesh.shape["win"] == 4
    return jax.shard_map(
        body if regular else plain_body,
        mesh=mesh,
        in_specs=(P("win", None, "pairs", None), P(), P(), P("win")),
        out_specs=P("win", "pairs", None, None),
        check_vma=False,
    )
```

```python
import functools
import math

import jax
import jax.numpy as jnp
from jax import lax
from jax.experimental import pallas as pl
from jax.experimental.pallas import tpu as pltpu
from jax.sharding import PartitionSpec as P

LAGS = 128
HALF = LAGS // 2
EPS = 1e-06
STEP = 16
WHITEN_VMEM = 60 << 20


def whiten_kernel(pairs_hbm, slot_hbm, offset_hbm, raw_hbm, *refs, scale):
    *outs, factor_ref, raw_ref, full, lead, pairs_ref, slot_ref, offset_ref, sems = refs
    slots, rows, rec = raw_ref.shape
    seg = rec - LAGS
    samples = seg - LAGS
    tiles = pairs_ref.shape[0]
    scalars = [
        pltpu.make_async_copy(src, dst, sems.at[i])
        for i, (src, dst) in enumerate(
            ((offset_hbm, offset_ref), (pairs_hbm, pairs_ref), (slot_hbm, slot_ref))
        )
    ]
    record = pltpu.make_async_copy(raw_hbm.at[0], raw_ref, sems.at[3])
    for one in [record] + scalars:
        one.start()
    owner = lax.axis_index("pairs")
    band = (
        jnp.abs(
            lax.broadcasted_iota(jnp.int32, (seg, seg), 0)
            - lax.broadcasted_iota(jnp.int32, (seg, seg), 1)
        )
        <= HALF
    ).astype(jnp.bfloat16)
    position = lax.broadcasted_iota(jnp.int32, (1, seg), 1)
    tally = jnp.minimum(position, HALF) + jnp.minimum(seg - 1 - position, HALF) + 1
    inverse = 1.0 / tally.astype(jnp.float32)
    scalars[0].wait()
    turn = lax.rem(rec - offset_ref[0], rec)
    record.wait()
    raw = raw_ref[...].reshape(slots * rows, rec)
    signal = pltpu.roll(raw.astype(jnp.float32), turn, 1)[:, :seg]
    running = jnp.dot(
        jnp.abs(signal).astype(jnp.bfloat16), band, preferred_element_type=jnp.float32
    )
    whitened = signal / (running * inverse + EPS)
    full[...] = whitened.astype(jnp.bfloat16).reshape(slots, rows, seg)
    lead[...] = whitened[:, HALF : HALF + samples].astype(jnp.bfloat16).reshape(slots, rows, samples)
    scalars[1].wait()
    scalars[2].wait()
    for t in range(tiles):
        used = jnp.where(pairs_ref[t, 0, owner] >= 0, scale, 0.0)
        factor_ref[t] = jnp.full(factor_ref.shape[1:], used, jnp.float32)
    for k, out in enumerate(outs):
        for t in range(tiles):
            first = slot_ref[jnp.maximum(pairs_ref[t, 0, owner ^ k], 0)]
            second = slot_ref[jnp.maximum(pairs_ref[t, 1, owner ^ k], 0)]
            out[t, :, :seg] = full[second]
            out[t, :, seg:] = lead[first]


def whiten_and_pack(raw_traces, pairs_last, block_slot, win_offset, scale):
    _, slots, rows, rec = raw_traces.shape
    tiles, _, owners = pairs_last.shape
    seg = rec - LAGS
    samples = seg - LAGS
    vmem = pl.BlockSpec(memory_space=pltpu.VMEM)
    return pl.pallas_call(
        functools.partial(whiten_kernel, scale=scale),
        in_specs=[pl.BlockSpec(memory_space=pl.ANY)] * 4,
        out_specs=[vmem] * (owners + 1),
        out_shape=[jax.ShapeDtypeStruct((tiles, rows, seg + samples), jnp.bfloat16)] * owners
        + [jax.ShapeDtypeStruct((tiles, 8, LAGS), jnp.float32)],
        scratch_shapes=[
            pltpu.VMEM((slots, rows, rec), jnp.bfloat16),
            pltpu.VMEM((slots, rows, seg), jnp.bfloat16),
            pltpu.VMEM((slots, rows, samples), jnp.bfloat16),
            pltpu.SMEM(pairs_last.shape, jnp.int32),
            pltpu.SMEM(block_slot.shape, jnp.int32),
            pltpu.SMEM(win_offset.shape, jnp.int32),
            pltpu.SemaphoreType.DMA((4,)),
        ],
        compiler_params=pltpu.CompilerParams(vmem_limit_bytes=WHITEN_VMEM),
        name="whiten",
    )(pairs_last, block_slot, win_offset, raw_traces)


def unit(far, near, owner, t, j, lanes):
    half, _, n, _ = near.shape
    k = owner ^ j
    here = (k < half).astype(jnp.int32) * jnp.ones((n, 1), jnp.int32) > 0
    at = k & (half - 1)
    return jnp.where(here, near[at, t, :, lanes], far[at, t, :, lanes])


def second_block(far, near, owner, t, lanes):
    return jnp.concatenate(
        [unit(far, near, owner, t, j, lanes) for j in range(2 * near.shape[0])], 0
    )


def first_rows(far, near, owner, share, t, rows, lanes):
    n = near.shape[2]
    return jnp.concatenate(
        [unit(far, near, owner, t, share * (rows // n) + j, lanes) for j in range(rows // n)], 0
    )


def turned(row):
    return pltpu.roll(jnp.broadcast_to(row, (STEP, LAGS)), 0, 1, stride=1, stride_axis=0)


def spread(c, lead, toeplitz, windows, samples):
    lane = lax.broadcasted_iota(jnp.int32, (STEP, LAGS), 1)
    early = lane < lax.broadcasted_iota(jnp.int32, (STEP, LAGS), 0)
    at = pl.ds(pl.multiple_of(c * STEP, STEP), STEP)
    for w in range(windows):
        before = 0.0
        row = lead[w, pl.ds(c, 1), :]
        for lo in range(0, samples, LAGS):
            now = turned(row[:, lo : lo + LAGS])
            toeplitz[at, w * samples + lo : w * samples + lo + LAGS] = jnp.where(
                early, before, now
            ).astype(jnp.bfloat16)
            before = now


def held_kernel(*refs, windows):
    far, near = refs[:windows], refs[windows : 2 * windows]
    out_ref, lead, *pairs_of = refs[2 * windows :]
    toeplitz, lagged = pairs_of[:2], pairs_of[2:]
    tiles, blocks, _, chans = out_ref.shape
    _, rows, samples = lead.shape
    seg = samples + LAGS
    rounds = blocks // 2
    per = rows // rounds
    owner, share = lax.axis_index("pairs"), lax.axis_index("win")
    for t in range(-1, tiles):
        if t + 1 < tiles:
            for w in range(windows):
                block = second_block(far[w], near[w], owner, t + 1, slice(0, seg))
                lagged[(t + 1) % 2][w] = block.T
                mine = first_rows(far[w], near[w], owner, share, t + 1, rows, slice(seg, None))
                lead[w] = mine.astype(jnp.float32)

        def step(q, _):
            if t >= 0:
                halves = []
                for b in range(2):
                    lo = pl.multiple_of((2 * q + b) * STEP, STEP)
                    parts = [lagged[t % 2][w, pl.ds(lo, samples), :] for w in range(windows)]
                    halves.append(jnp.concatenate(parts, 0))
                r = jnp.dot(
                    toeplitz[t % 2][...],
                    jnp.concatenate(halves, 1),
                    preferred_element_type=jnp.float32,
                )
                out_ref[t, 2 * q] = r[:, :chans]
                out_ref[t, 2 * q + 1] = r[:, chans:]
            if t + 1 < tiles:
                for i in range(per):
                    spread(q * per + i, lead, toeplitz[(t + 1) % 2], windows, samples)
            return 0

        lax.fori_loop(0, rounds, step, 0, unroll=True)


def stack_kernel(factor_hbm, *refs, windows):
    ins, sums, out_ref = refs[: 2 * windows], refs[2 * windows], refs[2 * windows + 1]
    far, near = ins[:windows], ins[windows:]
    lead, ends, *pairs_of, factor_ref, done, ready = refs[2 * windows + 2 :]
    toeplitz, lagged, lasting, product, staged = (pairs_of[i : i + 2] for i in range(0, 10, 2))
    rows, tiles, chans, _ = out_ref.shape
    new, _, samples = lead.shape
    seg = samples + LAGS
    wide = new * samples
    blocks = LAGS // STEP
    rounds = blocks // 2
    per = rows // rounds
    owner, share = lax.axis_index("pairs"), lax.axis_index("win")
    lane = lax.broadcasted_iota(jnp.int32, (STEP, LAGS), 1)
    shift = lax.broadcasted_iota(jnp.int32, (STEP, LAGS), 0)
    tail = (lax.rem(lane, STEP) < shift) & (lane < windows * STEP)
    factors = pltpu.make_async_copy(factor_hbm, factor_ref, ready.at[0])
    factors.start()

    def prepare(t, s):
        lanes = lax.broadcasted_iota(jnp.int32, (rows, LAGS), 1)
        last = jnp.zeros((rows, LAGS), jnp.float32)
        for w in range(windows):
            fresh = w - (windows - new)
            if fresh >= 0:
                lagged[s][fresh] = second_block(far[w], near[w], owner, t, slice(0, samples)).T
                mine = first_rows(
                    far[w], near[w], owner, share, t, rows, slice(seg, seg + samples)
                ).astype(jnp.float32)
                lead[fresh] = mine
                mine = mine[:, samples - LAGS :]
            else:
                mine = first_rows(
                    far[w], near[w], owner, share, t, rows, slice(2 * samples, None)
                ).astype(jnp.float32)
            lasting[s][w] = second_block(far[w], near[w], owner, t, slice(samples, seg)).T
            at = (w - 1) * STEP % LAGS
            last += jnp.where(
                (lanes >= at) & (lanes < at + STEP),
                pltpu.roll(mine, w * STEP, 1) if w else mine,
                0.0,
            )
        ends[...] = last

    def multiply(q, t, s):
        halves = []
        for b in range(2):
            lo = (2 * q + b) * STEP
            parts = []
            for w in range(new):
                parts += [lagged[s][w, lo:, :], lasting[s][windows - new + w, :lo, :]]
            parts += [lasting[s][w, lo : lo + STEP, :] for w in range(windows)]
            parts.append(jnp.zeros((LAGS - windows * STEP, chans), jnp.bfloat16))
            halves.append(jnp.concatenate([p for p in parts if p.shape[0]], 0))
        r = jnp.dot(
            toeplitz[s][...], jnp.concatenate(halves, 1), preferred_element_type=jnp.float32
        )
        product[s][2 * q] = r[:, :chans] + sums[t, 2 * q]
        product[s][2 * q + 1] = r[:, chans:] + sums[t, 2 * q + 1]

    def finish(c, s, factor):
        at = pl.ds(c * STEP, STEP)
        staged[s][c] = product[s][:, at, :].reshape(LAGS, chans).T * factor

    def copy(t):
        return pltpu.make_async_copy(staged[t % 2], out_ref.at[:, t], done.at[t % 2])

    for t in range(-1, tiles + 1):
        if t + 1 < tiles:
            prepare(t + 1, (t + 1) % 2)
        if t == 1:
            factors.wait()
        if t >= 1:
            factor = factor_ref[t - 1, 0:1, :]
            if t >= 3:
                copy(t - 3).wait()
        for q in range(rounds):
            if 0 <= t < tiles:
                multiply(q, t, t % 2)
            for c in range(q * per, (q + 1) * per):
                if t + 1 < tiles:
                    spread(c, lead, toeplitz[(t + 1) % 2], new, samples)
                    toeplitz[(t + 1) % 2][c * STEP : (c + 1) * STEP, wide:] = jnp.where(
                        tail, turned(ends[c : c + 1, :]), 0.0
                    ).astype(jnp.bfloat16)
                if t >= 1:
                    finish(c, (t - 1) % 2, factor)
        if t >= 1:
            copy(t - 1).start()
    for t in range(max(tiles - 2, 0), tiles):
        copy(t).wait()


def stack(factor, held, brought, rows, chans):
    _, tiles, n, width = held[0][0].shape
    samples = (width - LAGS) // 2
    seg = samples + LAGS
    depth = rows * STEP
    windows, old, new = len(held) + len(brought), len(held), len(brought)
    vmem = pl.BlockSpec(memory_space=pltpu.VMEM)
    hbm = pl.BlockSpec(memory_space=pl.ANY)

    def flat(groups):
        return [g[0] for g in groups] + [g[1] for g in groups]

    flops = 2 * tiles * depth * samples * chans * (LAGS // STEP)
    sums = pl.pallas_call(
        functools.partial(held_kernel, windows=old),
        in_specs=[vmem] * (2 * old),
        out_specs=vmem,
        out_shape=jax.ShapeDtypeStruct((tiles, LAGS // STEP, depth, chans), jnp.float32),
        scratch_shapes=[pltpu.VMEM((old, rows, samples), jnp.float32)]
        + [pltpu.VMEM((depth, old * samples), jnp.bfloat16)] * 2
        + [pltpu.VMEM((old, seg, chans), jnp.bfloat16)] * 2,
        compiler_params=pltpu.CompilerParams(vmem_limit_bytes=24 << 20),
        cost_estimate=pl.CostEstimate(
            flops=old * flops, bytes_accessed=8 << 20, transcendentals=0
        ),
        name="held",
    )(*flat(held))
    return pl.pallas_call(
        functools.partial(stack_kernel, windows=windows),
        in_specs=[hbm] + [vmem] * (2 * windows + 1),
        out_specs=hbm,
        out_shape=jax.ShapeDtypeStruct((rows, tiles, chans, LAGS), jnp.float32),
        scratch_shapes=[
            pltpu.VMEM((new, rows, samples), jnp.float32),
            pltpu.VMEM((rows, LAGS), jnp.float32),
        ]
        + [pltpu.VMEM((depth, new * samples + LAGS), jnp.bfloat16)] * 2
        + [pltpu.VMEM((new, samples, chans), jnp.bfloat16)] * 2
        + [pltpu.VMEM((windows, LAGS, chans), jnp.bfloat16)] * 2
        + [pltpu.VMEM((LAGS // STEP, depth, chans), jnp.float32)] * 2
        + [pltpu.VMEM((rows, chans, LAGS), jnp.float32)] * 2
        + [
            pltpu.VMEM(factor.shape, jnp.float32),
            pltpu.SemaphoreType.DMA((2,)),
            pltpu.SemaphoreType.DMA((1,)),
        ],
        compiler_params=pltpu.CompilerParams(vmem_limit_bytes=24 << 20),
        name="stack",
    )(factor, *flat(held + brought), sums)


def body(raw_traces, tile_pairs, block_slot, win_offset):
    owners = lax.axis_size("pairs")
    windows = lax.axis_size("win")
    rows, rec = raw_traces.shape[2:]
    chans = rows * owners
    samples = rec - 2 * LAGS
    pairs_last = jnp.transpose(tile_pairs, (1, 2, 0))
    scale = 1.0 / math.sqrt(windows * samples)
    *units, factor = whiten_and_pack(raw_traces, pairs_last, block_slot, win_offset, scale)

    def swap(x, axis, size, k):
        return lax.ppermute(x, axis, [(i, i ^ k) for i in range(size)])

    units = [u if k == 0 else swap(u, "pairs", owners, k) for k, u in enumerate(units)]
    held, brought = [], []
    for low in (owners // 2, 0):
        own = jnp.stack(units[low : low + owners // 2])
        other = swap(own, "win", windows, 2)
        held.append((own, swap(own, "win", windows, 1)))
        brought.append((other, swap(other, "win", windows, 1)))
    return stack(factor, list(zip(*held)), list(zip(*brought)), chans // windows, chans)


def plain_whiten(signal):
    length = signal.shape[-1]
    seg_count = length // LAGS
    magnitude = jnp.abs(signal).reshape(signal.shape[:-1] + (seg_count, LAGS))
    padded = jnp.pad(magnitude, [(0, 0)] * (magnitude.ndim - 2) + [(1, 1), (0, 0)])
    windows = jnp.concatenate([padded[..., :-2, :], padded[..., 1:-1, :], padded[..., 2:, :]], -1)
    rowpos = jnp.arange(3 * LAGS)[:, None]
    colpos = jnp.arange(LAGS)[None, :]
    band_matrix = (jnp.abs(rowpos - LAGS - colpos) <= HALF).astype(jnp.float32)
    totals = jnp.einsum(
        "...ni,ij->...nj", windows, band_matrix, precision=lax.Precision.HIGHEST
    ).reshape(signal.shape)
    position = jnp.arange(length)
    tally = (jnp.minimum(position, HALF) + jnp.minimum(length - 1 - position, HALF) + 1).astype(
        jnp.float32
    )
    return (signal / (totals / tally + EPS)).astype(jnp.bfloat16)


def plain_correlate(leading_blocks, trailing_blocks):
    seg_len = leading_blocks.shape[-1]
    samples = seg_len - LAGS
    kernel = jnp.transpose(leading_blocks[..., HALF : HALF + samples], (1, 0, 2))
    source = jnp.transpose(trailing_blocks[..., : seg_len - 1], (1, 0, 2))
    return lax.conv_general_dilated(
        source,
        kernel,
        (1,),
        "VALID",
        dimension_numbers=("NCH", "OIH", "CNH"),
        preferred_element_type=jnp.float32,
    )


def plain_body(raw_traces, tile_pairs, block_slot, win_offset):
    owner_index = lax.axis_index("pairs")
    pair_count = lax.axis_size("pairs")
    win_count = lax.axis_size("win")
    local_channels = raw_traces.shape[2]
    channels = local_channels * pair_count
    seg_len = raw_traces.shape[3] - LAGS
    samples = seg_len - LAGS
    tile_count = tile_pairs.shape[1]
    segment = lax.dynamic_slice_in_dim(raw_traces[0], win_offset[0], seg_len, 2).astype(jnp.float32)
    whitened = plain_whiten(segment)
    wanted = tile_pairs.reshape(pair_count, 2 * tile_count)
    slot_index = block_slot[jnp.maximum(wanted, 0)]
    outgoing = jnp.take(whitened, slot_index.reshape(-1), axis=0).reshape(
        pair_count, 2 * tile_count, local_channels, seg_len
    )
    incoming = lax.all_to_all(outgoing, "pairs", split_axis=0, concat_axis=2, tiled=True)
    blocks = incoming[0].reshape(tile_count, 2, channels, seg_len)
    own_tiles = lax.dynamic_index_in_dim(tile_pairs, owner_index, 0, keepdims=False)
    tile_valid = (own_tiles[:, 0] >= 0).astype(jnp.float32)
    firsts = blocks[:, 0]
    seconds = blocks[:, 1]
    spread_rows = lax.all_to_all(firsts[:, None], "win", split_axis=2, concat_axis=1, tiled=True)
    piece = lax.all_gather(seconds[:, None], "win", axis=1, tiled=True)
    summed = jnp.stack(
        [plain_correlate(spread_rows[tile], piece[tile]) for tile in range(tile_count)], 1
    )
    scale = 1.0 / math.sqrt(win_count * samples)
    return summed * scale * tile_valid[None, :, None, None]


def solution(mesh):
    regular = mesh.shape["pairs"] == 8 and mesh.shape["win"] == 4
    return jax.shard_map(
        body if regular else plain_body,
        mesh=mesh,
        in_specs=(P("win", None, "pairs", None), P(), P(), P("win")),
        out_specs=P("win", "pairs", None, None),
        check_vma=False,
    )
```

```python
import functools
import math

import jax
import jax.numpy as jnp
from jax import lax
from jax.experimental import pallas as pl
from jax.experimental.pallas import tpu as pltpu
from jax.sharding import PartitionSpec as P

LAGS = 128
HALF = LAGS // 2
EPS = 1e-06
STEP = 16
WHITEN_VMEM = 60 << 20
NEAR = (0, 1, 2, 4)
FAR = (3, 5, 6, 7)


def whiten_kernel(pairs_hbm, slot_hbm, offset_hbm, raw_hbm, *refs, scale):
    *outs, factor_ref, raw_ref, full, lead, pairs_ref, slot_ref, offset_ref, sems = refs
    slots, rows, rec = raw_ref.shape
    seg = rec - LAGS
    samples = seg - LAGS
    tiles = pairs_ref.shape[0]
    scalars = [
        pltpu.make_async_copy(src, dst, sems.at[i])
        for i, (src, dst) in enumerate(
            ((offset_hbm, offset_ref), (pairs_hbm, pairs_ref), (slot_hbm, slot_ref))
        )
    ]
    record = pltpu.make_async_copy(raw_hbm.at[0], raw_ref, sems.at[3])
    for one in [record] + scalars:
        one.start()
    owner = lax.axis_index("pairs")
    band = (
        jnp.abs(
            lax.broadcasted_iota(jnp.int32, (seg, seg), 0)
            - lax.broadcasted_iota(jnp.int32, (seg, seg), 1)
        )
        <= HALF
    ).astype(jnp.bfloat16)
    position = lax.broadcasted_iota(jnp.int32, (1, seg), 1)
    tally = jnp.minimum(position, HALF) + jnp.minimum(seg - 1 - position, HALF) + 1
    inverse = 1.0 / tally.astype(jnp.float32)
    scalars[0].wait()
    turn = lax.rem(rec - offset_ref[0], rec)
    record.wait()
    raw = raw_ref[...].reshape(slots * rows, rec)
    signal = pltpu.roll(raw.astype(jnp.float32), turn, 1)[:, :seg]
    running = jnp.dot(
        jnp.abs(signal).astype(jnp.bfloat16), band, preferred_element_type=jnp.float32
    )
    whitened = signal / (running * inverse + EPS)
    full[...] = whitened.astype(jnp.bfloat16).reshape(slots, rows, seg)
    lead[...] = whitened[:, HALF : HALF + samples].astype(jnp.bfloat16).reshape(slots, rows, samples)
    scalars[1].wait()
    scalars[2].wait()
    for t in range(tiles):
        used = jnp.where(pairs_ref[t, 0, owner] >= 0, scale, 0.0)
        factor_ref[t] = jnp.full(factor_ref.shape[1:], used, jnp.float32)
    for k, out in enumerate(outs):
        for t in range(tiles):
            first = slot_ref[jnp.maximum(pairs_ref[t, 0, owner ^ k], 0)]
            second = slot_ref[jnp.maximum(pairs_ref[t, 1, owner ^ k], 0)]
            out[t, :, :seg] = full[second]
            out[t, :, seg:] = lead[first]


def whiten_and_pack(raw_traces, pairs_last, block_slot, win_offset, scale):
    _, slots, rows, rec = raw_traces.shape
    tiles, _, owners = pairs_last.shape
    seg = rec - LAGS
    samples = seg - LAGS
    vmem = pl.BlockSpec(memory_space=pltpu.VMEM)
    return pl.pallas_call(
        functools.partial(whiten_kernel, scale=scale),
        in_specs=[pl.BlockSpec(memory_space=pl.ANY)] * 4,
        out_specs=[vmem] * (owners + 1),
        out_shape=[jax.ShapeDtypeStruct((tiles, rows, seg + samples), jnp.bfloat16)] * owners
        + [jax.ShapeDtypeStruct((tiles, 8, LAGS), jnp.float32)],
        scratch_shapes=[
            pltpu.VMEM((slots, rows, rec), jnp.bfloat16),
            pltpu.VMEM((slots, rows, seg), jnp.bfloat16),
            pltpu.VMEM((slots, rows, samples), jnp.bfloat16),
            pltpu.SMEM(pairs_last.shape, jnp.int32),
            pltpu.SMEM(block_slot.shape, jnp.int32),
            pltpu.SMEM(win_offset.shape, jnp.int32),
            pltpu.SemaphoreType.DMA((4,)),
        ],
        compiler_params=pltpu.CompilerParams(vmem_limit_bytes=WHITEN_VMEM),
        name="whiten",
    )(pairs_last, block_slot, win_offset, raw_traces)


def unit(far, near, owner, t, j, lanes):
    n = near.shape[2]
    k = owner ^ j
    here = ((k & (k - 1)) == 0).astype(jnp.int32) * jnp.ones((n, 1), jnp.int32) > 0
    in_near = jnp.minimum(k - (k >> 2), len(NEAR) - 1)
    in_far = jnp.maximum(k - len(NEAR), 0)
    return jnp.where(here, near[in_near, t, :, lanes], far[in_far, t, :, lanes])


def second_block(far, near, owner, t, lanes):
    return jnp.concatenate(
        [unit(far, near, owner, t, j, lanes) for j in range(2 * near.shape[0])], 0
    )


def first_rows(far, near, owner, share, t, rows, lanes):
    n = near.shape[2]
    return jnp.concatenate(
        [unit(far, near, owner, t, share * (rows // n) + j, lanes) for j in range(rows // n)], 0
    )


def turned(row):
    return pltpu.roll(jnp.broadcast_to(row, (STEP, LAGS)), 0, 1, stride=1, stride_axis=0)


def spread(c, lead, toeplitz, windows, samples):
    lane = lax.broadcasted_iota(jnp.int32, (STEP, LAGS), 1)
    early = lane < lax.broadcasted_iota(jnp.int32, (STEP, LAGS), 0)
    at = pl.ds(pl.multiple_of(c * STEP, STEP), STEP)
    for w in range(windows):
        before = 0.0
        row = lead[w, pl.ds(c, 1), :]
        for lo in range(0, samples, LAGS):
            now = turned(row[:, lo : lo + LAGS])
            toeplitz[at, w * samples + lo : w * samples + lo + LAGS] = jnp.where(
                early, before, now
            ).astype(jnp.bfloat16)
            before = now


def held_kernel(*refs, windows):
    far, near = refs[:windows], refs[windows : 2 * windows]
    out_ref, lead, *pairs_of = refs[2 * windows :]
    toeplitz, lagged = pairs_of[:2], pairs_of[2:]
    tiles, blocks, _, chans = out_ref.shape
    _, rows, samples = lead.shape
    seg = samples + LAGS
    rounds = blocks // 2
    per = rows // rounds
    owner, share = lax.axis_index("pairs"), lax.axis_index("win")
    for t in range(-1, tiles):
        if t + 1 < tiles:
            for w in range(windows):
                block = second_block(far[w], near[w], owner, t + 1, slice(0, seg))
                lagged[(t + 1) % 2][w] = block.T
                mine = first_rows(far[w], near[w], owner, share, t + 1, rows, slice(seg, None))
                lead[w] = mine.astype(jnp.float32)

        def step(q, _):
            if t >= 0:
                halves = []
                for b in range(2):
                    lo = pl.multiple_of((2 * q + b) * STEP, STEP)
                    parts = [lagged[t % 2][w, pl.ds(lo, samples), :] for w in range(windows)]
                    halves.append(jnp.concatenate(parts, 0))
                r = jnp.dot(
                    toeplitz[t % 2][...],
                    jnp.concatenate(halves, 1),
                    preferred_element_type=jnp.float32,
                )
                out_ref[t, 2 * q] = r[:, :chans]
                out_ref[t, 2 * q + 1] = r[:, chans:]
            if t + 1 < tiles:
                for i in range(per):
                    spread(q * per + i, lead, toeplitz[(t + 1) % 2], windows, samples)
            return 0

        lax.fori_loop(0, rounds, step, 0, unroll=True)


def stack_kernel(factor_hbm, *refs, windows):
    ins, sums, out_ref = refs[: 2 * windows], refs[2 * windows], refs[2 * windows + 1]
    far, near = ins[:windows], ins[windows:]
    lead, ends, *pairs_of, factor_ref, done, ready = refs[2 * windows + 2 :]
    toeplitz, lagged, lasting, product, staged = (pairs_of[i : i + 2] for i in range(0, 10, 2))
    rows, tiles, chans, _ = out_ref.shape
    new, _, samples = lead.shape
    seg = samples + LAGS
    wide = new * samples
    blocks = LAGS // STEP
    rounds = blocks // 2
    per = rows // rounds
    owner, share = lax.axis_index("pairs"), lax.axis_index("win")
    lane = lax.broadcasted_iota(jnp.int32, (STEP, LAGS), 1)
    shift = lax.broadcasted_iota(jnp.int32, (STEP, LAGS), 0)
    tail = (lax.rem(lane, STEP) < shift) & (lane < windows * STEP)
    factors = pltpu.make_async_copy(factor_hbm, factor_ref, ready.at[0])
    factors.start()

    def prepare(t, s):
        lanes = lax.broadcasted_iota(jnp.int32, (rows, LAGS), 1)
        last = jnp.zeros((rows, LAGS), jnp.float32)
        for w in range(windows):
            fresh = w - (windows - new)
            if fresh >= 0:
                lagged[s][fresh] = second_block(far[w], near[w], owner, t, slice(0, samples)).T
                mine = first_rows(
                    far[w], near[w], owner, share, t, rows, slice(seg, seg + samples)
                ).astype(jnp.float32)
                lead[fresh] = mine
                mine = mine[:, samples - LAGS :]
            else:
                mine = first_rows(
                    far[w], near[w], owner, share, t, rows, slice(2 * samples, None)
                ).astype(jnp.float32)
            lasting[s][w] = second_block(far[w], near[w], owner, t, slice(samples, seg)).T
            at = (w - 1) * STEP % LAGS
            last += jnp.where(
                (lanes >= at) & (lanes < at + STEP),
                pltpu.roll(mine, w * STEP, 1) if w else mine,
                0.0,
            )
        ends[...] = last

    def multiply(q, t, s):
        halves = []
        for b in range(2):
            lo = (2 * q + b) * STEP
            parts = []
            for w in range(new):
                parts += [lagged[s][w, lo:, :], lasting[s][windows - new + w, :lo, :]]
            parts += [lasting[s][w, lo : lo + STEP, :] for w in range(windows)]
            parts.append(jnp.zeros((LAGS - windows * STEP, chans), jnp.bfloat16))
            halves.append(jnp.concatenate([p for p in parts if p.shape[0]], 0))
        r = jnp.dot(
            toeplitz[s][...], jnp.concatenate(halves, 1), preferred_element_type=jnp.float32
        )
        product[s][2 * q] = r[:, :chans] + sums[t, 2 * q]
        product[s][2 * q + 1] = r[:, chans:] + sums[t, 2 * q + 1]

    def finish(c, s, factor):
        at = pl.ds(c * STEP, STEP)
        staged[s][c] = product[s][:, at, :].reshape(LAGS, chans).T * factor

    def copy(t):
        return pltpu.make_async_copy(staged[t % 2], out_ref.at[:, t], done.at[t % 2])

    for t in range(-1, tiles + 1):
        if t + 1 < tiles:
            prepare(t + 1, (t + 1) % 2)
        if t == 1:
            factors.wait()
        if t >= 1:
            factor = factor_ref[t - 1, 0:1, :]
            if t >= 3:
                copy(t - 3).wait()
        for q in range(rounds):
            if 0 <= t < tiles:
                multiply(q, t, t % 2)
            for c in range(q * per, (q + 1) * per):
                if t + 1 < tiles:
                    spread(c, lead, toeplitz[(t + 1) % 2], new, samples)
                    toeplitz[(t + 1) % 2][c * STEP : (c + 1) * STEP, wide:] = jnp.where(
                        tail, turned(ends[c : c + 1, :]), 0.0
                    ).astype(jnp.bfloat16)
                if t >= 1:
                    finish(c, (t - 1) % 2, factor)
        if t >= 1:
            copy(t - 1).start()
    for t in range(max(tiles - 2, 0), tiles):
        copy(t).wait()


def stack(factor, held, brought, rows, chans):
    _, tiles, n, width = held[0][0].shape
    samples = (width - LAGS) // 2
    seg = samples + LAGS
    depth = rows * STEP
    windows, old, new = len(held) + len(brought), len(held), len(brought)
    vmem = pl.BlockSpec(memory_space=pltpu.VMEM)
    hbm = pl.BlockSpec(memory_space=pl.ANY)

    def flat(groups):
        return [g[0] for g in groups] + [g[1] for g in groups]

    flops = 2 * tiles * depth * samples * chans * (LAGS // STEP)
    sums = pl.pallas_call(
        functools.partial(held_kernel, windows=old),
        in_specs=[vmem] * (2 * old),
        out_specs=vmem,
        out_shape=jax.ShapeDtypeStruct((tiles, LAGS // STEP, depth, chans), jnp.float32),
        scratch_shapes=[pltpu.VMEM((old, rows, samples), jnp.float32)]
        + [pltpu.VMEM((depth, old * samples), jnp.bfloat16)] * 2
        + [pltpu.VMEM((old, seg, chans), jnp.bfloat16)] * 2,
        compiler_params=pltpu.CompilerParams(vmem_limit_bytes=24 << 20),
        cost_estimate=pl.CostEstimate(
            flops=old * flops, bytes_accessed=8 << 20, transcendentals=0
        ),
        name="held",
    )(*flat(held))
    return pl.pallas_call(
        functools.partial(stack_kernel, windows=windows),
        in_specs=[hbm] + [vmem] * (2 * windows + 1),
        out_specs=hbm,
        out_shape=jax.ShapeDtypeStruct((rows, tiles, chans, LAGS), jnp.float32),
        scratch_shapes=[
            pltpu.VMEM((new, rows, samples), jnp.float32),
            pltpu.VMEM((rows, LAGS), jnp.float32),
        ]
        + [pltpu.VMEM((depth, new * samples + LAGS), jnp.bfloat16)] * 2
        + [pltpu.VMEM((new, samples, chans), jnp.bfloat16)] * 2
        + [pltpu.VMEM((windows, LAGS, chans), jnp.bfloat16)] * 2
        + [pltpu.VMEM((LAGS // STEP, depth, chans), jnp.float32)] * 2
        + [pltpu.VMEM((rows, chans, LAGS), jnp.float32)] * 2
        + [
            pltpu.VMEM(factor.shape, jnp.float32),
            pltpu.SemaphoreType.DMA((2,)),
            pltpu.SemaphoreType.DMA((1,)),
        ],
        compiler_params=pltpu.CompilerParams(vmem_limit_bytes=24 << 20),
        name="stack",
    )(factor, *flat(held + brought), sums)


def body(raw_traces, tile_pairs, block_slot, win_offset):
    owners = lax.axis_size("pairs")
    windows = lax.axis_size("win")
    rows, rec = raw_traces.shape[2:]
    chans = rows * owners
    samples = rec - 2 * LAGS
    pairs_last = jnp.transpose(tile_pairs, (1, 2, 0))
    scale = 1.0 / math.sqrt(windows * samples)
    *units, factor = whiten_and_pack(raw_traces, pairs_last, block_slot, win_offset, scale)

    def swap(x, axis, size, k):
        return lax.ppermute(x, axis, [(i, i ^ k) for i in range(size)])

    units = [u if k == 0 else swap(u, "pairs", owners, k) for k, u in enumerate(units)]
    held, brought = [], []
    for group in (FAR, NEAR):
        own = jnp.stack([units[k] for k in group])
        other = swap(own, "win", windows, 2)
        held.append((own, swap(own, "win", windows, 1)))
        brought.append((other, swap(other, "win", windows, 1)))
    return stack(factor, list(zip(*held)), list(zip(*brought)), chans // windows, chans)


def plain_whiten(signal):
    length = signal.shape[-1]
    seg_count = length // LAGS
    magnitude = jnp.abs(signal).reshape(signal.shape[:-1] + (seg_count, LAGS))
    padded = jnp.pad(magnitude, [(0, 0)] * (magnitude.ndim - 2) + [(1, 1), (0, 0)])
    windows = jnp.concatenate([padded[..., :-2, :], padded[..., 1:-1, :], padded[..., 2:, :]], -1)
    rowpos = jnp.arange(3 * LAGS)[:, None]
    colpos = jnp.arange(LAGS)[None, :]
    band_matrix = (jnp.abs(rowpos - LAGS - colpos) <= HALF).astype(jnp.float32)
    totals = jnp.einsum(
        "...ni,ij->...nj", windows, band_matrix, precision=lax.Precision.HIGHEST
    ).reshape(signal.shape)
    position = jnp.arange(length)
    tally = (jnp.minimum(position, HALF) + jnp.minimum(length - 1 - position, HALF) + 1).astype(
        jnp.float32
    )
    return (signal / (totals / tally + EPS)).astype(jnp.bfloat16)


def plain_correlate(leading_blocks, trailing_blocks):
    seg_len = leading_blocks.shape[-1]
    samples = seg_len - LAGS
    kernel = jnp.transpose(leading_blocks[..., HALF : HALF + samples], (1, 0, 2))
    source = jnp.transpose(trailing_blocks[..., : seg_len - 1], (1, 0, 2))
    return lax.conv_general_dilated(
        source,
        kernel,
        (1,),
        "VALID",
        dimension_numbers=("NCH", "OIH", "CNH"),
        preferred_element_type=jnp.float32,
    )


def plain_body(raw_traces, tile_pairs, block_slot, win_offset):
    owner_index = lax.axis_index("pairs")
    pair_count = lax.axis_size("pairs")
    win_count = lax.axis_size("win")
    local_channels = raw_traces.shape[2]
    channels = local_channels * pair_count
    seg_len = raw_traces.shape[3] - LAGS
    samples = seg_len - LAGS
    tile_count = tile_pairs.shape[1]
    segment = lax.dynamic_slice_in_dim(raw_traces[0], win_offset[0], seg_len, 2).astype(jnp.float32)
    whitened = plain_whiten(segment)
    wanted = tile_pairs.reshape(pair_count, 2 * tile_count)
    slot_index = block_slot[jnp.maximum(wanted, 0)]
    outgoing = jnp.take(whitened, slot_index.reshape(-1), axis=0).reshape(
        pair_count, 2 * tile_count, local_channels, seg_len
    )
    incoming = lax.all_to_all(outgoing, "pairs", split_axis=0, concat_axis=2, tiled=True)
    blocks = incoming[0].reshape(tile_count, 2, channels, seg_len)
    own_tiles = lax.dynamic_index_in_dim(tile_pairs, owner_index, 0, keepdims=False)
    tile_valid = (own_tiles[:, 0] >= 0).astype(jnp.float32)
    firsts = blocks[:, 0]
    seconds = blocks[:, 1]
    spread_rows = lax.all_to_all(firsts[:, None], "win", split_axis=2, concat_axis=1, tiled=True)
    piece = lax.all_gather(seconds[:, None], "win", axis=1, tiled=True)
    summed = jnp.stack(
        [plain_correlate(spread_rows[tile], piece[tile]) for tile in range(tile_count)], 1
    )
    scale = 1.0 / math.sqrt(win_count * samples)
    return summed * scale * tile_valid[None, :, None, None]


def solution(mesh):
    regular = mesh.shape["pairs"] == 8 and mesh.shape["win"] == 4
    return jax.shard_map(
        body if regular else plain_body,
        mesh=mesh,
        in_specs=(P("win", None, "pairs", None), P(), P(), P("win")),
        out_specs=P("win", "pairs", None, None),
        check_vma=False,
    )
```
